32 devices in a mesh: aa: 4 (over z), ba: 2 (over core), col: 4 (over y, x).
Axes of the slice: x: 2, y: 2, z: 4, core: 2. Of those that a mesh axis runs over, the one named last changes fastest.
Arguments:
- density: float32 [128, 64, 512], P('aa', 'ba', 'col'), may hold values from 0.1 to 2
- lower_coupling: float32 [128, 64, 512], P('aa', 'ba', 'col'), may hold values from 0.005 to 40000
- upper_coupling: float32 [128, 64, 512], P('aa', 'ba', 'col'), may hold values from 0.005 to 40000
- reaction: float32 [128, 64, 512], P('aa', 'ba', 'col'), may hold values from 0.5 to 2
- cross_weight: float32 [128, 64, 512], P('aa', 'ba', 'col'), may hold values from -1 to 1
Outputs:
- new_density: float32 [128, 64, 512], P('aa', 'ba', 'col')
The draws below stay inside these ranges and needn't reach their ends.
All inputs are finite; a program needn't handle non-finite values.
Results may differ from the reference program's by a relative error of at most 0.0019.
Values sent between devices are 32-bit elements; how exact they have to be, the bound alone decides.
A program may use at most 64 MiB of HBM per device.

```python
import math
import jax
import jax.numpy as jnp
from jax import lax

NA = 128
NB = 64
NC = 512


def line_scale(key):
    exponent = jax.random.uniform(key, (NB, NC), jnp.float32, math.log(0.01), math.log(20000.0))
    return jnp.exp(exponent)


def cell_factor(key):
    exponent = jax.random.uniform(key, (NA, NB, NC), jnp.float32, math.log(0.5), math.log(2.0))
    return jnp.exp(exponent)


def draw_lower_coupling(key, part):
    scale = line_scale(key)
    key = jax.random.fold_in(key, 11)
    return (scale[None] * cell_factor(key)).astype(jnp.float32)


def draw_upper_coupling(key, part):
    scale = line_scale(key)
    key = jax.random.fold_in(key, 23)
    return (scale[None] * cell_factor(key)).astype(jnp.float32)


def steps_of(rng, shape, shards, smallest, high):
    def one(axis_at, shards_of):
        draws = jax.random.uniform(jax.random.fold_in(jax.random.fold_in(rng, 6), axis_at), (shards_of,), jnp.float32, smallest / len(shards), high / len(shards))
        return jnp.repeat(jnp.exp(draws), shape[axis_at] // shards_of).reshape((-1,) + (1,) * (len(shape) - axis_at - 1))

    level = one(*shards[0])
    for cut in shards[1:]:
        level = level * one(*cut)
    return level


def setup_inputs(seed: int = 0) -> dict:
    splits = jax.random.split(jax.random.key(seed), 6)
    density = jnp.clip(0.1 + 1.9 * jax.random.uniform(splits[0], (NA, NB, NC), jnp.float32) ** steps_of(splits[0], (NA, NB, NC), ((0, 4), (1, 2), (2, 4)), -0.2, 0.2), 0.1, 2.0)
    lower_coupling = draw_lower_coupling(jax.random.fold_in(splits[5], 71), 0)
    upper_coupling = draw_upper_coupling(jax.random.fold_in(splits[5], 71), 0)
    reaction = jnp.clip(jnp.exp(math.log(2.0) - 1.3862944 * jax.random.uniform(splits[3], (NA, NB, NC), jnp.float32) ** steps_of(splits[3], (NA, NB, NC), ((0, 4), (1, 2), (2, 4)), -0.2, 0.2)), 0.5, 2.0)
    cross_weight = jnp.clip(jax.random.uniform(splits[4], (NA, NB, NC), jnp.float32, -1.0, 1.0) * steps_of(splits[4], (NA, NB, NC), ((0, 4), (1, 2), (2, 4)), -0.4, 0.0), -1.0, 1.0)
    return {"density": density, "lower_coupling": lower_coupling, "upper_coupling": upper_coupling, "reaction": reaction, "cross_weight": cross_weight}


def cross_term(density, cross_weight):
    padded = jnp.pad(density, ((0, 0), (1, 1), (1, 1)))
    mixture = padded[:, 2:, 2:] - padded[:, 2:, :-2] - padded[:, :-2, 2:] + padded[:, :-2, :-2]
    return cross_weight * mixture


def reference(density, lower_coupling, upper_coupling, reaction, cross_weight):
    right_side = density + cross_term(density, cross_weight)
    diagonal = reaction + lower_coupling + upper_coupling

    def forward_row(carry, inputs):
        ratio, offset = carry
        low_row, up_row, diag_row, side_row = inputs
        denominator = diag_row + low_row * ratio
        new_ratio = -up_row / denominator
        new_offset = (side_row + low_row * offset) / denominator
        return (new_ratio, new_offset), (new_ratio, new_offset)

    start = jnp.zeros(density.shape[1:], jnp.float32)
    unused, (ratios, offsets) = lax.scan(forward_row, (start, start), (lower_coupling, upper_coupling, diagonal, right_side))

    def backward_row(carry, inputs):
        ratio, offset = inputs
        value = offset - ratio * carry
        return value, value

    unused_last, values = lax.scan(backward_row, start, (ratios, offsets), reverse=True)
    return values
```

```python
import functools

import jax
import jax.numpy as jnp
from jax import lax
from jax.experimental import pallas as pl
from jax.experimental.pallas import tpu as pltpu
from jax.sharding import PartitionSpec as P

MESH = pl.DeviceIdType.MESH
SUB, LANES = 8, 128


def kernel(
    line, cols, p_hbm, l_hbm, u_hbm, s_hbm, w_hbm, x_hbm,
    p, l, u, s, w, x, t, r, f, o, b,
    edge_out, edge_in, row_out, row_in, mat_out, mat_in, rhs_out, rhs_in, res_out, res_in,
    load_sem, store_sem, edge_send, edge_recv, row_send, row_recv,
    mat_send, mat_recv, rhs_send, rhs_recv, res_send, res_recv,
):
    rows, width, _ = p.shape
    half = rows // 2
    tiles = width // SUB
    aa, ba, col = lax.axis_index("aa"), lax.axis_index("ba"), lax.axis_index("col")
    other = 1 - ba
    left, right = lax.rem(col + cols - 1, cols), lax.rem(col + 1, cols)

    loads = [
        pltpu.make_async_copy(src, dst, load_sem.at[i])
        for i, (src, dst) in enumerate(((p_hbm, p), (l_hbm, l), (u_hbm, u), (s_hbm, s), (w_hbm, w)))
    ]
    for load in loads:
        load.start()

    barrier = pltpu.get_barrier_semaphore()
    beside = [(aa, other, col)] + [(aa, half_b, c) for c in (left, right) for half_b in (ba, other)]
    along = [(lax.rem(aa + d, line), ba, col) for d in range(1, line)]
    for device in beside + along:
        pl.semaphore_signal(barrier, inc=1, device_id=device, device_id_type=MESH)

    def send(src, dst, send_sem, recv_sem, device):
        return pltpu.make_async_remote_copy(
            src_ref=src, dst_ref=dst, send_sem=send_sem, recv_sem=recv_sem,
            device_id=device, device_id_type=MESH,
        )

    lane = lax.broadcasted_iota(jnp.int32, (SUB, LANES), 1)
    sub = lax.broadcasted_iota(jnp.int32, (SUB, LANES), 0)
    plane_lane = lax.broadcasted_iota(jnp.int32, (width, LANES), 1)
    plane_sub = lax.broadcasted_iota(jnp.int32, (width, LANES), 0)
    lower_half = (ba == 0).astype(jnp.float32)
    upper_half = 1.0 - lower_half

    loads[0].wait()
    parts = []
    for k in range(tiles):
        last = jnp.zeros((SUB, LANES), jnp.float32)
        first = last
        for a in range(rows):
            j = k * rows + a
            moved = pltpu.roll(p[a, k * SUB : (k + 1) * SUB, :], (j + 1) % LANES, 1)
            last = jnp.where(lane == j, moved, last)
            first = jnp.where(lane == (j + 1) % LANES, moved, first)
        parts.append((last, first))
    last = functools.reduce(jnp.add, [part[0] for part in parts])
    first = functools.reduce(jnp.add, [part[1] for part in parts])
    edge_out[0] = last
    edge_out[1] = pltpu.roll(first, LANES - 1, 1)
    row_out[...] = jnp.where(ba == 0, p[:, width - 1, :], p[:, 0, :])

    pl.semaphore_wait(barrier, len(beside) + len(along))

    halo = [send(row_out, row_in, row_send, row_recv, (aa, other, col))]
    for side, target in ((0, right), (1, left)):
        for which, half_b in ((0, ba), (1, other)):
            i = 2 * side + which
            halo.append(
                send(edge_out.at[side], edge_in.at[i], edge_send.at[i], edge_recv.at[i], (aa, half_b, target))
            )
    for copy in halo:
        copy.start()

    for load in loads[1:4]:
        load.wait()
    ends = []
    for order, outer, inner in (
        (tuple(range(half)), l, u),
        (tuple(range(rows - 1, half - 1, -1)), u, l),
    ):
        ends.append([order, outer, inner, None, None, None, None])
    for i in range(half):
        for end in ends:
            order, outer, inner, keep, fill, far, run = end
            a = order[i]
            excess = s[a] + (outer[a] if keep is None else outer[a] * keep)
            scale = 1.0 / (excess + inner[a])
            ratio = inner[a] * scale
            weight = outer[a] * scale
            keep = excess * scale
            fill = weight if fill is None else weight * fill
            t[a], r[a], f[a] = scale, ratio, fill
            far = fill if far is None else far + run * fill
            run = ratio if run is None else run * ratio
            end[3:] = [keep, fill, far, run]
    (keep1, f1, far1, run1), (keep2, f2, far2, run2) = ends[0][3:], ends[1][3:]
    r1, r2 = r[half - 1], r[half]
    joint = 1.0 / (keep1 + r1 * keep2)
    link1, link2 = run1 * joint, run2 * joint
    spikes = (far1 + link1 * (r2 * f1), link1 * f2, link2 * f1, far2 + link2 * (r1 * f2))
    for i, spike in enumerate(spikes):
        for k in range(tiles):
            mat_out[k, i] = spike[k * SUB : (k + 1) * SUB]

    stride = line // tiles
    mine = aa // stride
    solves = None if stride == 1 else lax.rem(aa, stride) == 0

    def solver_only(body):
        if solves is None:
            body()
        else:
            pl.when(solves)(body)

    def to_solvers(out, into, send_sem, recv_sem, act):
        def one(d):
            k = lax.rem(mine + d, tiles)
            act(send(out.at[k], into.at[aa], send_sem.at[k], recv_sem.at[aa], (k * stride, ba, col)))

        for d in range(1, tiles):
            one(d)
        if solves is not None:
            pl.when(jnp.logical_not(solves))(lambda: one(0))

    def from_line(into, send_sem, recv_sem):
        for d in range(1, line):
            j = lax.rem(aa + d, line)
            send(into.at[j], into.at[j], send_sem.at[0], recv_sem.at[j], (j, ba, col)).wait_recv()

    to_solvers(mat_out, mat_in, mat_send, mat_recv, lambda copy: copy.start())

    loads[4].wait()

    def across(value, lanes):
        after = jnp.where(lanes < LANES - 1, pltpu.roll(value, LANES - 1, 1), 0.0)
        return after - jnp.where(lanes > 0, pltpu.roll(value, 1, 1), 0.0)

    for a in range(rows):
        value = p[a]
        step = across(value, plane_lane)
        mixed = jnp.where(plane_sub < width - 1, pltpu.roll(step, width - 1, 0), 0.0)
        mixed = mixed - jnp.where(plane_sub > 0, pltpu.roll(step, 1, 0), 0.0)
        b[a] = value + w[a] * mixed

    for copy in halo:
        copy.wait_recv()

    def column(same, opposite):
        def up(value):
            return pltpu.roll(value, SUB - 1, 0)

        def down(value):
            return pltpu.roll(value, 1, 0)

        ahead = jnp.where(
            lane < LANES - rows,
            pltpu.roll(up(same), LANES - rows, 1),
            pltpu.roll(up(opposite), LANES - rows, 1) * lower_half,
        )
        behind = jnp.where(
            lane >= rows, pltpu.roll(down(same), rows, 1), pltpu.roll(down(opposite), rows, 1) * upper_half
        )
        return jnp.where(sub < SUB - 1, up(same), ahead) - jnp.where(sub > 0, down(same), behind)

    from_left = column(edge_in[0], edge_in[1]) * jnp.where(col > 0, -1.0, 0.0)
    from_right = column(edge_in[2], edge_in[3]) * jnp.where(col < cols - 1, 1.0, 0.0)
    from_left = pltpu.roll(from_left, 1, 1)
    odd = lax.rem(lane, 2) == 1
    pairs = (jnp.where(odd, from_left, from_right), jnp.where(odd, from_right, from_left))
    at_edge = jnp.logical_or(lane == 0, lane == LANES - 1)
    row_step = across(row_in[...], lax.broadcasted_iota(jnp.int32, (rows, LANES), 1))
    row_in[...] = row_step * (lower_half - upper_half)

    def side(a):
        line_in = row_in[a : a + 1, :]
        terms = []
        for k in range(tiles):
            term = jnp.where(at_edge, pltpu.roll(pairs[a % 2], (LANES - 1 - k * rows - a) % LANES, 1), 0.0)
            if k == 0:
                term = term + jnp.where(sub == 0, line_in * upper_half, 0.0)
            if k == tiles - 1:
                term = term + jnp.where(sub == SUB - 1, line_in * lower_half, 0.0)
            terms.append(term)
        return b[a] + w[a] * jnp.concatenate(terms, axis=0)

    state = [[None, None, None], [None, None, None]]
    for i in range(half):
        for end, held in zip(ends, state):
            order, outer = end[0], end[1]
            a = order[i]
            offset, far, run = held
            offset = side(a) * t[a] if offset is None else (side(a) + outer[a] * offset) * t[a]
            o[a] = offset
            far = offset if far is None else far + run * offset
            run = r[a] if run is None else run * r[a]
            held[:] = [offset, far, run]
    (o1, far1, _), (o2, far2, _) = state
    for i, value in enumerate((far1 + link1 * (o2 + r2 * o1), far2 + link2 * (o1 + r1 * o2))):
        for k in range(tiles):
            rhs_out[k, i] = value[k * SUB : (k + 1) * SUB]
    to_solvers(rhs_out, rhs_in, rhs_send, rhs_recv, lambda copy: copy.start())

    def reduced():
        mat_in[aa] = mat_out[mine]
        rhs_in[aa] = rhs_out[mine]
        from_line(mat_in, mat_send, mat_recv)
        slope = []
        before = jnp.zeros((SUB, LANES), jnp.float32)
        for j in range(line):
            first_l, first_r, last_l, last_r = (mat_in[j, i] for i in range(4))
            inverse = 1.0 / (1.0 - first_l * before)
            slope.append((before, inverse, inverse * first_r, first_l, last_l))
            before = last_r + last_l * before * slope[j][2]
        from_line(rhs_in, rhs_send, rhs_recv)
        base = []
        shift = jnp.zeros((SUB, LANES), jnp.float32)
        for j in range(line):
            before, inverse, _, first_l, last_l = slope[j]
            start = inverse * (rhs_in[j, 0] + first_l * shift)
            base.append((shift, start))
            shift = rhs_in[j, 1] + last_l * (shift + before * start)
        after = jnp.zeros((SUB, LANES), jnp.float32)
        for j in range(line - 1, -1, -1):
            res_out[j, 1] = after
            after = base[j][1] + slope[j][2] * after
            res_out[j, 0] = base[j][0] + slope[j][0] * after
        for d in range(1, line):
            j = lax.rem(aa + d, line)
            send(res_out.at[j], res_in.at[mine], res_send.at[j], res_recv.at[mine], (j, ba, col)).start()
        res_in[mine] = res_out[aa]

    solver_only(reduced)

    def from_solver(d):
        k = lax.rem(mine + d, tiles)
        send(
            res_in.at[k], res_in.at[k], res_send.at[0], res_recv.at[k], (k * stride, ba, col)
        ).wait_recv()

    for d in range(1, tiles):
        from_solver(d)
    if solves is not None:
        pl.when(jnp.logical_not(solves))(lambda: from_solver(0))

    before = jnp.concatenate([res_in[k, 0] for k in range(tiles)], axis=0)
    after = jnp.concatenate([res_in[k, 1] for k in range(tiles)], axis=0)
    top, bottom = o[half - 1] + f[half - 1] * before, o[half] + f[half] * after
    upper, lower = joint * (top + r1 * bottom), joint * (bottom + r2 * top)
    x[half - 1], x[half] = upper, lower
    for i in range(1, half):
        a, c = half - 1 - i, half + i
        upper = (o[a] + f[a] * before) + r[a] * upper
        lower = (o[c] + f[c] * after) + r[c] * lower
        x[a], x[c] = upper, lower
    store = pltpu.make_async_copy(x, x_hbm, store_sem)
    store.start()

    for copy in halo:
        copy.wait_send()
    to_solvers(mat_out, mat_in, mat_send, mat_recv, lambda copy: copy.wait_send())
    to_solvers(rhs_out, rhs_in, rhs_send, rhs_recv, lambda copy: copy.wait_send())

    def results_sent():
        for d in range(1, line):
            j = lax.rem(aa + d, line)
            send(
                res_out.at[j], res_in.at[mine], res_send.at[j], res_recv.at[mine], (j, ba, col)
            ).wait_send()

    solver_only(results_sent)
    store.wait()


def shards(line, cols, density, lower_coupling, upper_coupling, reaction, cross_weight):
    rows, width, lanes = density.shape
    tiles = width // SUB
    assert lanes == LANES and rows * tiles == LANES and line % tiles == 0
    block = pltpu.VMEM((rows, width, lanes), jnp.float32)

    def tile(*lead):
        return pltpu.VMEM((*lead, SUB, LANES), jnp.float32)

    dma = pltpu.SemaphoreType.DMA
    return pl.pallas_call(
        functools.partial(kernel, line, cols),
        out_shape=jax.ShapeDtypeStruct(density.shape, jnp.float32),
        in_specs=[pl.BlockSpec(memory_space=pl.ANY)] * 5,
        out_specs=pl.BlockSpec(memory_space=pl.ANY),
        scratch_shapes=[block] * 11
        + [
            tile(2),
            tile(4),
            pltpu.VMEM((rows, lanes), jnp.float32),
            pltpu.VMEM((rows, lanes), jnp.float32),
            tile(tiles, 4),
            tile(line, 4),
            tile(tiles, 2),
            tile(line, 2),
            tile(line, 2),
            tile(tiles, 2),
            dma((5,)),
            dma,
            dma((4,)),
            dma((4,)),
            dma,
            dma,
            dma((tiles,)),
            dma((line,)),
            dma((tiles,)),
            dma((line,)),
            dma((line,)),
            dma((tiles,)),
        ],
        compiler_params=pltpu.CompilerParams(
            collective_id=0, has_side_effects=True, vmem_limit_bytes=32 * 1024 * 1024
        ),
    )(density, lower_coupling, upper_coupling, reaction, cross_weight)


def solution(mesh):
    spec = P("aa", "ba", "col")
    body = functools.partial(shards, mesh.shape["aa"], mesh.shape["col"])
    return jax.shard_map(body, mesh=mesh, in_specs=(spec,) * 5, out_specs=spec, check_vma=False)
```

```python
import functools

import jax
import jax.numpy as jnp
from jax import lax
from jax.experimental import pallas as pl
from jax.experimental.pallas import tpu as pltpu
from jax.sharding import PartitionSpec as P

MESH = pl.DeviceIdType.MESH
SUB, LANES = 8, 128


def kernel(
    line, cols, p_hbm, l_hbm, u_hbm, s_hbm, w_hbm, x,
    p, l, u, s, w, t, r, f, o, b,
    edge_out, edge_in, row_out, row_in, mat_out, mat_in, rhs_out, rhs_in, res_out, res_in,
    load_sem, edge_send, edge_recv, row_send, row_recv,
    mat_send, mat_recv, rhs_send, rhs_recv, res_send, res_recv,
):
    rows, width, _ = p.shape
    half = rows // 2
    tiles = width // SUB
    aa, ba, col = lax.axis_index("aa"), lax.axis_index("ba"), lax.axis_index("col")
    other = 1 - ba
    left, right = lax.rem(col + cols - 1, cols), lax.rem(col + 1, cols)

    loads = [
        pltpu.make_async_copy(src, dst, load_sem.at[i])
        for i, (src, dst) in enumerate(((p_hbm, p), (l_hbm, l), (u_hbm, u), (s_hbm, s), (w_hbm, w)))
    ]
    for load in loads:
        load.start()

    barrier = pltpu.get_barrier_semaphore()
    beside = [(aa, other, col)] + [(aa, half_b, c) for c in (left, right) for half_b in (ba, other)]
    along = [(lax.rem(aa + d, line), ba, col) for d in range(1, line)]
    for device in beside + along:
        pl.semaphore_signal(barrier, inc=1, device_id=device, device_id_type=MESH)

    def send(src, dst, send_sem, recv_sem, device):
        return pltpu.make_async_remote_copy(
            src_ref=src, dst_ref=dst, send_sem=send_sem, recv_sem=recv_sem,
            device_id=device, device_id_type=MESH,
        )

    lane = lax.broadcasted_iota(jnp.int32, (SUB, LANES), 1)
    sub = lax.broadcasted_iota(jnp.int32, (SUB, LANES), 0)
    plane_lane = lax.broadcasted_iota(jnp.int32, (width, LANES), 1)
    plane_sub = lax.broadcasted_iota(jnp.int32, (width, LANES), 0)
    lower_half = (ba == 0).astype(jnp.float32)
    upper_half = 1.0 - lower_half

    loads[0].wait()
    parts = []
    for k in range(tiles):
        last = jnp.zeros((SUB, LANES), jnp.float32)
        first = last
        for a in range(rows):
            j = k * rows + a
            moved = pltpu.roll(p[a, k * SUB : (k + 1) * SUB, :], (j + 1) % LANES, 1)
            last = jnp.where(lane == j, moved, last)
            first = jnp.where(lane == (j + 1) % LANES, moved, first)
        parts.append((last, first))
    last = functools.reduce(jnp.add, [part[0] for part in parts])
    first = functools.reduce(jnp.add, [part[1] for part in parts])
    edge_out[0] = last
    edge_out[1] = pltpu.roll(first, LANES - 1, 1)
    row_out[...] = jnp.where(ba == 0, p[:, width - 1, :], p[:, 0, :])

    pl.semaphore_wait(barrier, len(beside) + len(along))

    halo = [send(row_out, row_in, row_send, row_recv, (aa, other, col))]
    for side, target in ((0, right), (1, left)):
        for which, half_b in ((0, ba), (1, other)):
            i = 2 * side + which
            halo.append(
                send(edge_out.at[side], edge_in.at[i], edge_send.at[i], edge_recv.at[i], (aa, half_b, target))
            )
    for copy in halo:
        copy.start()

    for load in loads[1:4]:
        load.wait()
    ends = []
    for order, outer, inner in (
        (tuple(range(half)), l, u),
        (tuple(range(rows - 1, half - 1, -1)), u, l),
    ):
        ends.append([order, outer, inner, None, None, None, None])
    for i in range(half):
        for end in ends:
            order, outer, inner, keep, fill, far, run = end
            a = order[i]
            excess = s[a] + (outer[a] if keep is None else outer[a] * keep)
            scale = 1.0 / (excess + inner[a])
            ratio = inner[a] * scale
            weight = outer[a] * scale
            keep = excess * scale
            fill = weight if fill is None else weight * fill
            t[a], r[a], f[a] = scale, ratio, fill
            far = fill if far is None else far + run * fill
            run = ratio if run is None else run * ratio
            end[3:] = [keep, fill, far, run]
    (keep1, f1, far1, run1), (keep2, f2, far2, run2) = ends[0][3:], ends[1][3:]
    r1, r2 = r[half - 1], r[half]
    joint = 1.0 / (keep1 + r1 * keep2)
    link1, link2 = run1 * joint, run2 * joint
    spikes = (far1 + link1 * (r2 * f1), link1 * f2, link2 * f1, far2 + link2 * (r1 * f2))
    for i, spike in enumerate(spikes):
        for k in range(tiles):
            mat_out[k, i] = spike[k * SUB : (k + 1) * SUB]

    stride = line // tiles
    mine = aa // stride
    solves = None if stride == 1 else lax.rem(aa, stride) == 0

    def solver_only(body):
        if solves is None:
            body()
        else:
            pl.when(solves)(body)

    def to_solvers(out, into, send_sem, recv_sem, act):
        def one(d):
            k = lax.rem(mine + d, tiles)
            act(send(out.at[k], into.at[aa], send_sem.at[k], recv_sem.at[aa], (k * stride, ba, col)))

        for d in range(1, tiles):
            one(d)
        if solves is not None:
            pl.when(jnp.logical_not(solves))(lambda: one(0))

    def from_line(into, send_sem, recv_sem):
        for d in range(1, line):
            j = lax.rem(aa + d, line)
            send(into.at[j], into.at[j], send_sem.at[0], recv_sem.at[j], (j, ba, col)).wait_recv()

    to_solvers(mat_out, mat_in, mat_send, mat_recv, lambda copy: copy.start())

    loads[4].wait()

    def across(value, lanes):
        after = jnp.where(lanes < LANES - 1, pltpu.roll(value, LANES - 1, 1), 0.0)
        return after - jnp.where(lanes > 0, pltpu.roll(value, 1, 1), 0.0)

    for a in range(rows):
        value = p[a]
        step = across(value, plane_lane)
        mixed = jnp.where(plane_sub < width - 1, pltpu.roll(step, width - 1, 0), 0.0)
        mixed = mixed - jnp.where(plane_sub > 0, pltpu.roll(step, 1, 0), 0.0)
        b[a] = value + w[a] * mixed

    for copy in halo:
        copy.wait_recv()

    def column(same, opposite):
        def up(value):
            return pltpu.roll(value, SUB - 1, 0)

        def down(value):
            return pltpu.roll(value, 1, 0)

        ahead = jnp.where(
            lane < LANES - rows,
            pltpu.roll(up(same), LANES - rows, 1),
            pltpu.roll(up(opposite), LANES - rows, 1) * lower_half,
        )
        behind = jnp.where(
            lane >= rows, pltpu.roll(down(same), rows, 1), pltpu.roll(down(opposite), rows, 1) * upper_half
        )
        return jnp.where(sub < SUB - 1, up(same), ahead) - jnp.where(sub > 0, down(same), behind)

    from_left = column(edge_in[0], edge_in[1]) * jnp.where(col > 0, -1.0, 0.0)
    from_right = column(edge_in[2], edge_in[3]) * jnp.where(col < cols - 1, 1.0, 0.0)
    from_left = pltpu.roll(from_left, 1, 1)
    odd = lax.rem(lane, 2) == 1
    pairs = (jnp.where(odd, from_left, from_right), jnp.where(odd, from_right, from_left))
    at_edge = jnp.logical_or(lane == 0, lane == LANES - 1)
    row_step = across(row_in[...], lax.broadcasted_iota(jnp.int32, (rows, LANES), 1))
    row_in[...] = row_step * (lower_half - upper_half)

    def side(a):
        line_in = row_in[a : a + 1, :]
        terms = []
        for k in range(tiles):
            term = jnp.where(at_edge, pltpu.roll(pairs[a % 2], (LANES - 1 - k * rows - a) % LANES, 1), 0.0)
            if k == 0:
                term = term + jnp.where(sub == 0, line_in * upper_half, 0.0)
            if k == tiles - 1:
                term = term + jnp.where(sub == SUB - 1, line_in * lower_half, 0.0)
            terms.append(term)
        return b[a] + w[a] * jnp.concatenate(terms, axis=0)

    state = [[None, None, None], [None, None, None]]
    for i in range(half):
        for end, held in zip(ends, state):
            order, outer = end[0], end[1]
            a = order[i]
            offset, far, run = held
            offset = side(a) * t[a] if offset is None else (side(a) + outer[a] * offset) * t[a]
            o[a] = offset
            far = offset if far is None else far + run * offset
            run = r[a] if run is None else run * r[a]
            held[:] = [offset, far, run]
    (o1, far1, _), (o2, far2, _) = state
    for i, value in enumerate((far1 + link1 * (o2 + r2 * o1), far2 + link2 * (o1 + r1 * o2))):
        for k in range(tiles):
            rhs_out[k, i] = value[k * SUB : (k + 1) * SUB]
    to_solvers(rhs_out, rhs_in, rhs_send, rhs_recv, lambda copy: copy.start())

    def reduced():
        mat_in[aa] = mat_out[mine]
        rhs_in[aa] = rhs_out[mine]
        from_line(mat_in, mat_send, mat_recv)
        slope = []
        before = jnp.zeros((SUB, LANES), jnp.float32)
        for j in range(line):
            first_l, first_r, last_l, last_r = (mat_in[j, i] for i in range(4))
            inverse = 1.0 / (1.0 - first_l * before)
            slope.append((before, inverse, inverse * first_r, first_l, last_l))
            before = last_r + last_l * before * slope[j][2]
        from_line(rhs_in, rhs_send, rhs_recv)
        base = []
        shift = jnp.zeros((SUB, LANES), jnp.float32)
        for j in range(line):
            before, inverse, _, first_l, last_l = slope[j]
            start = inverse * (rhs_in[j, 0] + first_l * shift)
            base.append((shift, start))
            shift = rhs_in[j, 1] + last_l * (shift + before * start)
        after = jnp.zeros((SUB, LANES), jnp.float32)
        for j in range(line - 1, -1, -1):
            res_out[j, 1] = after
            after = base[j][1] + slope[j][2] * after
            res_out[j, 0] = base[j][0] + slope[j][0] * after
        for d in range(1, line):
            j = lax.rem(aa + d, line)
            send(res_out.at[j], res_in.at[mine], res_send.at[j], res_recv.at[mine], (j, ba, col)).start()
        res_in[mine] = res_out[aa]

    solver_only(reduced)

    def from_solver(d):
        k = lax.rem(mine + d, tiles)
        send(
            res_in.at[k], res_in.at[k], res_send.at[0], res_recv.at[k], (k * stride, ba, col)
        ).wait_recv()

    for d in range(1, tiles):
        from_solver(d)
    if solves is not None:
        pl.when(jnp.logical_not(solves))(lambda: from_solver(0))

    before = jnp.concatenate([res_in[k, 0] for k in range(tiles)], axis=0)
    after = jnp.concatenate([res_in[k, 1] for k in range(tiles)], axis=0)
    top, bottom = o[half - 1] + f[half - 1] * before, o[half] + f[half] * after
    upper, lower = joint * (top + r1 * bottom), joint * (bottom + r2 * top)
    x[half - 1], x[half] = upper, lower
    for i in range(1, half):
        a, c = half - 1 - i, half + i
        upper = (o[a] + f[a] * before) + r[a] * upper
        lower = (o[c] + f[c] * after) + r[c] * lower
        x[a], x[c] = upper, lower

    for copy in halo:
        copy.wait_send()
    to_solvers(mat_out, mat_in, mat_send, mat_recv, lambda copy: copy.wait_send())
    to_solvers(rhs_out, rhs_in, rhs_send, rhs_recv, lambda copy: copy.wait_send())

    def results_sent():
        for d in range(1, line):
            j = lax.rem(aa + d, line)
            send(
                res_out.at[j], res_in.at[mine], res_send.at[j], res_recv.at[mine], (j, ba, col)
            ).wait_send()

    solver_only(results_sent)


def shards(line, cols, density, lower_coupling, upper_coupling, reaction, cross_weight):
    rows, width, lanes = density.shape
    tiles = width // SUB
    assert lanes == LANES and rows * tiles == LANES and line % tiles == 0
    block = pltpu.VMEM((rows, width, lanes), jnp.float32)

    def tile(*lead):
        return pltpu.VMEM((*lead, SUB, LANES), jnp.float32)

    dma = pltpu.SemaphoreType.DMA
    return pl.pallas_call(
        functools.partial(kernel, line, cols),
        out_shape=pltpu.VMEM(density.shape, jnp.float32),
        in_specs=[pl.BlockSpec(memory_space=pl.ANY)] * 5,
        out_specs=pl.BlockSpec(memory_space=pltpu.VMEM),
        scratch_shapes=[block] * 10
        + [
            tile(2),
            tile(4),
            pltpu.VMEM((rows, lanes), jnp.float32),
            pltpu.VMEM((rows, lanes), jnp.float32),
            tile(tiles, 4),
            tile(line, 4),
            tile(tiles, 2),
            tile(line, 2),
            tile(line, 2),
            tile(tiles, 2),
            dma((5,)),
            dma((4,)),
            dma((4,)),
            dma,
            dma,
            dma((tiles,)),
            dma((line,)),
            dma((tiles,)),
            dma((line,)),
            dma((line,)),
            dma((tiles,)),
        ],
        compiler_params=pltpu.CompilerParams(
            collective_id=0, has_side_effects=True, vmem_limit_bytes=55 * 1024 * 1024
        ),
    )(density, lower_coupling, upper_coupling, reaction, cross_weight)


def solution(mesh):
    spec = P("aa", "ba", "col")
    body = functools.partial(shards, mesh.shape["aa"], mesh.shape["col"])
    return jax.shard_map(body, mesh=mesh, in_specs=(spec,) * 5, out_specs=spec, check_vma=False)
```

```python
import functools

import jax
import jax.numpy as jnp
from jax import lax
from jax.experimental import pallas as pl
from jax.experimental.pallas import tpu as pltpu
from jax.sharding import PartitionSpec as P

MESH = pl.DeviceIdType.MESH
SUB, LANES = 8, 128


def kernel(
    line, cols, p_hbm, l_hbm, u_hbm, s_hbm, w_hbm, x,
    p, l, u, s, w, t, r, f, o, b,
    edge_out, edge_in, row_out, row_in, mat_out, mat_in, rhs_out, rhs_in, res_out, res_in,
    load_sem, edge_send, edge_recv, row_send, row_recv,
    mat_send, mat_recv, rhs_send, rhs_recv, res_send, res_recv,
):
    rows, width, _ = p.shape
    half = rows // 2
    tiles = width // SUB
    aa, ba, col = lax.axis_index("aa"), lax.axis_index("ba"), lax.axis_index("col")
    other = 1 - ba
    left, right = lax.rem(col + cols - 1, cols), lax.rem(col + 1, cols)

    loads = [
        pltpu.make_async_copy(src, dst, load_sem.at[i])
        for i, (src, dst) in enumerate(((p_hbm, p), (l_hbm, l), (u_hbm, u), (s_hbm, s), (w_hbm, w)))
    ]
    for load in loads:
        load.start()

    barrier = pltpu.get_barrier_semaphore()
    beside = [(aa, other, col)] + [(aa, half_b, c) for c in (left, right) for half_b in (ba, other)]
    along = [(lax.rem(aa + d, line), ba, col) for d in range(1, line)]
    for device in beside + along:
        pl.semaphore_signal(barrier, inc=1, device_id=device, device_id_type=MESH)

    def send(src, dst, send_sem, recv_sem, device):
        return pltpu.make_async_remote_copy(
            src_ref=src, dst_ref=dst, send_sem=send_sem, recv_sem=recv_sem,
            device_id=device, device_id_type=MESH,
        )

    lane = lax.broadcasted_iota(jnp.int32, (SUB, LANES), 1)
    sub = lax.broadcasted_iota(jnp.int32, (SUB, LANES), 0)
    plane_lane = lax.broadcasted_iota(jnp.int32, (width, LANES), 1)
    plane_sub = lax.broadcasted_iota(jnp.int32, (width, LANES), 0)
    lower_half = (ba == 0).astype(jnp.float32)
    upper_half = 1.0 - lower_half

    loads[0].wait()
    parts = []
    for k in range(tiles):
        last = jnp.zeros((SUB, LANES), jnp.float32)
        first = last
        for a in range(rows):
            j = k * rows + a
            moved = pltpu.roll(p[a, k * SUB : (k + 1) * SUB, :], (j + 1) % LANES, 1)
            last = jnp.where(lane == j, moved, last)
            first = jnp.where(lane == (j + 1) % LANES, moved, first)
        parts.append((last, first))
    last = functools.reduce(jnp.add, [part[0] for part in parts])
    first = functools.reduce(jnp.add, [part[1] for part in parts])
    edge_out[0] = last
    edge_out[1] = pltpu.roll(first, LANES - 1, 1)
    row_out[...] = jnp.where(ba == 0, p[:, width - 1, :], p[:, 0, :])

    pl.semaphore_wait(barrier, len(beside) + len(along))

    halo = [send(row_out, row_in, row_send, row_recv, (aa, other, col))]
    for side, target in ((0, right), (1, left)):
        for which, half_b in ((0, ba), (1, other)):
            i = 2 * side + which
            halo.append(
                send(edge_out.at[side], edge_in.at[i], edge_send.at[i], edge_recv.at[i], (aa, half_b, target))
            )
    for copy in halo:
        copy.start()

    for load in loads[1:4]:
        load.wait()
    ends = []
    for order, outer, inner in (
        (tuple(range(half)), l, u),
        (tuple(range(rows - 1, half - 1, -1)), u, l),
    ):
        ends.append([order, outer, inner, None, None, None, None])
    for i in range(half):
        for end in ends:
            order, outer, inner, keep, fill, far, run = end
            a = order[i]
            excess = s[a] + (outer[a] if keep is None else outer[a] * keep)
            scale = 1.0 / (excess + inner[a])
            ratio = inner[a] * scale
            weight = outer[a] * scale
            keep = excess * scale
            fill = weight if fill is None else weight * fill
            t[a], r[a], f[a] = scale, ratio, fill
            outer[a] = weight
            far = fill if far is None else far + run * fill
            run = ratio if run is None else run * ratio
            end[3:] = [keep, fill, far, run]
    (keep1, f1, far1, run1), (keep2, f2, far2, run2) = ends[0][3:], ends[1][3:]
    r1, r2 = r[half - 1], r[half]
    joint = 1.0 / (keep1 + r1 * keep2)
    link1, link2 = run1 * joint, run2 * joint
    spikes = (far1 + link1 * (r2 * f1), link1 * f2, link2 * f1, far2 + link2 * (r1 * f2))
    for i, spike in enumerate(spikes):
        for k in range(tiles):
            mat_out[k, i] = spike[k * SUB : (k + 1) * SUB]

    stride = line // tiles
    mine = aa // stride
    solves = None if stride == 1 else lax.rem(aa, stride) == 0

    def solver_only(body):
        if solves is None:
            body()
        else:
            pl.when(solves)(body)

    def to_solvers(out, into, send_sem, recv_sem, act):
        def one(d):
            k = lax.rem(mine + d, tiles)
            act(send(out.at[k], into.at[aa], send_sem.at[k], recv_sem.at[aa], (k * stride, ba, col)))

        for d in range(1, tiles):
            one(d)
        if solves is not None:
            pl.when(jnp.logical_not(solves))(lambda: one(0))

    def from_line(into, send_sem, recv_sem):
        for d in range(1, line):
            j = lax.rem(aa + d, line)
            send(into.at[j], into.at[j], send_sem.at[0], recv_sem.at[j], (j, ba, col)).wait_recv()

    to_solvers(mat_out, mat_in, mat_send, mat_recv, lambda copy: copy.start())

    loads[4].wait()

    def across(value, lanes):
        after = jnp.where(lanes < LANES - 1, pltpu.roll(value, LANES - 1, 1), 0.0)
        return after - jnp.where(lanes > 0, pltpu.roll(value, 1, 1), 0.0)

    for a in range(rows):
        value = p[a]
        step = across(value, plane_lane)
        mixed = jnp.where(plane_sub < width - 1, pltpu.roll(step, width - 1, 0), 0.0)
        mixed = mixed - jnp.where(plane_sub > 0, pltpu.roll(step, 1, 0), 0.0)
        b[a] = (value + w[a] * mixed) * t[a]
        w[a] = w[a] * t[a]

    for copy in halo:
        copy.wait_recv()

    def column(same, opposite):
        def up(value):
            return pltpu.roll(value, SUB - 1, 0)

        def down(value):
            return pltpu.roll(value, 1, 0)

        ahead = jnp.where(
            lane < LANES - rows,
            pltpu.roll(up(same), LANES - rows, 1),
            pltpu.roll(up(opposite), LANES - rows, 1) * lower_half,
        )
        behind = jnp.where(
            lane >= rows, pltpu.roll(down(same), rows, 1), pltpu.roll(down(opposite), rows, 1) * upper_half
        )
        return jnp.where(sub < SUB - 1, up(same), ahead) - jnp.where(sub > 0, down(same), behind)

    from_left = column(edge_in[0], edge_in[1]) * jnp.where(col > 0, -1.0, 0.0)
    from_right = column(edge_in[2], edge_in[3]) * jnp.where(col < cols - 1, 1.0, 0.0)
    from_left = pltpu.roll(from_left, 1, 1)
    odd = lax.rem(lane, 2) == 1
    pairs = (jnp.where(odd, from_left, from_right), jnp.where(odd, from_right, from_left))
    at_edge = jnp.logical_or(lane == 0, lane == LANES - 1)
    row_step = across(row_in[...], lax.broadcasted_iota(jnp.int32, (rows, LANES), 1))
    row_in[...] = row_step * (lower_half - upper_half)

    def side(a):
        line_in = row_in[a : a + 1, :]
        terms = []
        for k in range(tiles):
            term = jnp.where(at_edge, pltpu.roll(pairs[a % 2], (LANES - 1 - k * rows - a) % LANES, 1), 0.0)
            if k == 0:
                term = term + jnp.where(sub == 0, line_in * upper_half, 0.0)
            if k == tiles - 1:
                term = term + jnp.where(sub == SUB - 1, line_in * lower_half, 0.0)
            terms.append(term)
        return b[a] + w[a] * jnp.concatenate(terms, axis=0)

    state = [[None, None, None], [None, None, None]]
    for i in range(half):
        for end, held in zip(ends, state):
            order, outer = end[0], end[1]
            a = order[i]
            offset, far, run = held
            offset = side(a) if offset is None else side(a) + outer[a] * offset
            o[a] = offset
            far = offset if far is None else far + run * offset
            run = r[a] if run is None else run * r[a]
            held[:] = [offset, far, run]
    (o1, far1, _), (o2, far2, _) = state
    for i, value in enumerate((far1 + link1 * (o2 + r2 * o1), far2 + link2 * (o1 + r1 * o2))):
        for k in range(tiles):
            rhs_out[k, i] = value[k * SUB : (k + 1) * SUB]
    to_solvers(rhs_out, rhs_in, rhs_send, rhs_recv, lambda copy: copy.start())

    def reduced():
        mat_in[aa] = mat_out[mine]
        rhs_in[aa] = rhs_out[mine]
        from_line(mat_in, mat_send, mat_recv)
        slope = []
        before = jnp.zeros((SUB, LANES), jnp.float32)
        for j in range(line):
            first_l, first_r, last_l, last_r = (mat_in[j, i] for i in range(4))
            inverse = 1.0 / (1.0 - first_l * before)
            slope.append((before, inverse, inverse * first_r, first_l, last_l))
            before = last_r + last_l * before * slope[j][2]
        from_line(rhs_in, rhs_send, rhs_recv)
        base = []
        shift = jnp.zeros((SUB, LANES), jnp.float32)
        for j in range(line):
            before, inverse, _, first_l, last_l = slope[j]
            start = inverse * (rhs_in[j, 0] + first_l * shift)
            base.append((shift, start))
            shift = rhs_in[j, 1] + last_l * (shift + before * start)
        after = jnp.zeros((SUB, LANES), jnp.float32)
        for j in range(line - 1, -1, -1):
            res_out[j, 1] = after
            after = base[j][1] + slope[j][2] * after
            res_out[j, 0] = base[j][0] + slope[j][0] * after
        for d in range(1, line):
            j = lax.rem(aa + d, line)
            send(res_out.at[j], res_in.at[mine], res_send.at[j], res_recv.at[mine], (j, ba, col)).start()
        res_in[mine] = res_out[aa]

    solver_only(reduced)

    def from_solver(d):
        k = lax.rem(mine + d, tiles)
        send(
            res_in.at[k], res_in.at[k], res_send.at[0], res_recv.at[k], (k * stride, ba, col)
        ).wait_recv()

    for d in range(1, tiles):
        from_solver(d)
    if solves is not None:
        pl.when(jnp.logical_not(solves))(lambda: from_solver(0))

    before = jnp.concatenate([res_in[k, 0] for k in range(tiles)], axis=0)
    after = jnp.concatenate([res_in[k, 1] for k in range(tiles)], axis=0)
    top, bottom = o[half - 1] + f[half - 1] * before, o[half] + f[half] * after
    upper, lower = joint * (top + r1 * bottom), joint * (bottom + r2 * top)
    x[half - 1], x[half] = upper, lower
    for i in range(1, half):
        a, c = half - 1 - i, half + i
        upper = (o[a] + f[a] * before) + r[a] * upper
        lower = (o[c] + f[c] * after) + r[c] * lower
        x[a], x[c] = upper, lower

    for copy in halo:
        copy.wait_send()
    to_solvers(mat_out, mat_in, mat_send, mat_recv, lambda copy: copy.wait_send())
    to_solvers(rhs_out, rhs_in, rhs_send, rhs_recv, lambda copy: copy.wait_send())

    def results_sent():
        for d in range(1, line):
            j = lax.rem(aa + d, line)
            send(
                res_out.at[j], res_in.at[mine], res_send.at[j], res_recv.at[mine], (j, ba, col)
            ).wait_send()

    solver_only(results_sent)


def shards(line, cols, density, lower_coupling, upper_coupling, reaction, cross_weight):
    rows, width, lanes = density.shape
    tiles = width // SUB
    assert lanes == LANES and rows * tiles == LANES and line % tiles == 0
    block = pltpu.VMEM((rows, width, lanes), jnp.float32)

    def tile(*lead):
        return pltpu.VMEM((*lead, SUB, LANES), jnp.float32)

    dma = pltpu.SemaphoreType.DMA
    return pl.pallas_call(
        functools.partial(kernel, line, cols),
        out_shape=pltpu.VMEM(density.shape, jnp.float32),
        in_specs=[pl.BlockSpec(memory_space=pl.ANY)] * 5,
        out_specs=pl.BlockSpec(memory_space=pltpu.VMEM),
        scratch_shapes=[block] * 10
        + [
            tile(2),
            tile(4),
            pltpu.VMEM((rows, lanes), jnp.float32),
            pltpu.VMEM((rows, lanes), jnp.float32),
            tile(tiles, 4),
            tile(line, 4),
            tile(tiles, 2),
            tile(line, 2),
            tile(line, 2),
            tile(tiles, 2),
            dma((5,)),
            dma((4,)),
            dma((4,)),
            dma,
            dma,
            dma((tiles,)),
            dma((line,)),
            dma((tiles,)),
            dma((line,)),
            dma((line,)),
            dma((tiles,)),
        ],
        compiler_params=pltpu.CompilerParams(
            collective_id=0, has_side_effects=True, vmem_limit_bytes=55 * 1024 * 1024
        ),
    )(density, lower_coupling, upper_coupling, reaction, cross_weight)


def solution(mesh):
    spec = P("aa", "ba", "col")
    body = functools.partial(shards, mesh.shape["aa"], mesh.shape["col"])
    return jax.shard_map(body, mesh=mesh, in_specs=(spec,) * 5, out_specs=spec, check_vma=False)
```
